1024 devices in a mesh: edata: 8 (over z), node: 16 (over x, core), local: 8 (over y).
Axes of the slice: x: 8, y: 8, z: 8, core: 2. Of those that a mesh axis runs over, the one named last changes fastest.
Arguments:
- tokens: bfloat16 [8192, 2048], P(('edata', 'node', 'local')), may hold values from -6 to 6
- cotangent: bfloat16 [8192, 2048], P(('edata', 'node', 'local')), may hold values from -6 to 6
- expert_ids: int32 [8192, 8], P(('edata', 'node', 'local')), may hold values from 0 to 127, as said below
- route_weights: bfloat16 [8192, 8], P(('edata', 'node', 'local')), may hold values from 0.049804688 to 0.5
- w_gate: bfloat16 [128, 2048, 768], P(('node', 'local')), may hold values from -0.125 to 0.125
- w_up: bfloat16 [128, 2048, 768], P(('node', 'local')), may hold values from -0.125 to 0.125
- w_down: bfloat16 [128, 768, 2048], P(('node', 'local')), may hold values from -0.21875 to 0.21875
Outputs:
- token_grad: bfloat16 [8192, 2048], P(('edata', 'node', 'local'))
- weight_grad: bfloat16 [8192, 8], P(('edata', 'node', 'local'))
- down_grad: float32 [128, 768, 2048], P(('node', 'local'), 'edata')
The draws below stay inside these ranges and needn't reach their ends.
Inputs may be any that keep to these rules, and one draw needn't show every extreme that they name: `expert_ids`: each row names 8 different experts. Within the 128 tokens of the devices that share their edata and local indices, every expert is named by 0 or exactly 16 tokens, and one expert is named by 16 tokens in every such set.
All inputs are finite; a program needn't handle non-finite values.
Results may differ from the reference program's by a relative error of at most 0.015.
Values may be sent and summed in bfloat16 or wider, within the bound.
A program may use at most 64 MiB of HBM per device.

```python
import math
import jax
import jax.numpy as jnp
from jax import lax

D = 2048
FF = 768
TOP = 8
TOK_DEV = 8
REPLICAS = 8
NODE_GROUPS = 16
GROUP_EXPERTS = 8
EXPERTS = 128
TOKENS = 8192
COLUMN = 128
SLOTS = 16
USED = 64


def draw_expert_ids(key, part):
    key = jax.random.fold_in(key, 7)
    key_hot, key_pick, key_place = jax.random.split(key, 3)
    groups = REPLICAS * GROUP_EXPERTS
    hottest = jax.random.randint(key_hot, (), 0, EXPERTS).astype(jnp.int32)
    others = jax.vmap(lambda subkey: jax.random.permutation(subkey, EXPERTS - 1))(jax.random.split(key_pick, groups))
    others = (hottest + 1 + others[:, :USED - 1].astype(jnp.int32)) % EXPERTS
    chosen = jnp.concatenate([jnp.full((groups, 1), hottest, jnp.int32), others], axis=1)
    places = jax.vmap(lambda subkey: jax.random.permutation(subkey, COLUMN))(jax.random.split(key_place, groups))
    residue = (places.astype(jnp.int32)[:, :, None] + jnp.arange(TOP, dtype=jnp.int32)[None, None, :]) % USED
    routes = jnp.take_along_axis(chosen, residue.reshape(groups, COLUMN * TOP), axis=1)
    routes = routes.reshape(REPLICAS, GROUP_EXPERTS, NODE_GROUPS, TOK_DEV, TOP)
    routes = routes.transpose(0, 2, 1, 3, 4).reshape(TOKENS, TOP)
    return routes.astype(jnp.int32)


def block_scale(key, shape, cuts, least, largest):
    def one(dim, blocks):
        heights = jax.random.uniform(jax.random.fold_in(jax.random.fold_in(key, 6), dim), (blocks,), jnp.float32, least / len(cuts), largest / len(cuts))
        return jnp.repeat(jnp.exp(heights), shape[dim] // blocks).reshape((-1,) + (1,) * (len(shape) - dim - 1))

    gain = one(*cuts[0])
    for cut in cuts[1:]:
        gain = gain * one(*cut)
    return gain


def centred(own_key, shape, scale, limit, pieces=(), held_as=jnp.bfloat16):
    drawn = scale * jax.random.normal(own_key, shape, jnp.float32)
    if pieces:
        drawn = drawn * block_scale(own_key, shape, pieces, -0.22, 0.18)
    return jnp.clip(drawn, -limit, limit).astype(held_as)


def setup_inputs(seed: int = 0) -> dict:
    keys = jax.random.split(jax.random.key(seed), 8)
    return {
        "tokens": centred(keys[0], (TOKENS, D), 1.0, 6.0, ((0, 1024),)),
        "cotangent": centred(keys[1], (TOKENS, D), 1.0, 6.0, ((0, 1024),)),
        "expert_ids": draw_expert_ids(jax.random.fold_in(keys[7], 71), 0),
        "route_weights": jnp.clip(jnp.exp(math.log(0.5) - 2.306499 * jax.random.uniform(keys[3], (TOKENS, TOP), jnp.float32) ** block_scale(keys[3], (TOKENS, TOP), ((0, 1024),), -0.2, 0.2)), 0.049804688, 0.5).astype(jnp.bfloat16),
        "w_gate": centred(keys[4], (EXPERTS, D, FF), D ** -0.5, 0.125, ((0, 128),)),
        "w_up": centred(keys[5], (EXPERTS, D, FF), D ** -0.5, 0.125, ((0, 128),)),
        "w_down": centred(keys[6], (EXPERTS, FF, D), FF ** -0.5, 0.21875, ((0, 128),)),
    }


def expert_pass(rows, grads, weight_col, gate_weight, up_weight, down_weight):
    gate_value = jnp.dot(rows, gate_weight, preferred_element_type=jnp.float32)
    up_value = jnp.dot(rows, up_weight, preferred_element_type=jnp.float32)
    sigmoid_gate = jax.nn.sigmoid(gate_value)
    silu_gate = gate_value * sigmoid_gate
    hidden = (silu_gate * up_value).astype(jnp.bfloat16)
    output = jnp.dot(hidden, down_weight, preferred_element_type=jnp.float32)
    weight_slot = jnp.sum(grads.astype(jnp.float32) * output, axis=1).astype(jnp.bfloat16)
    out_grad = (weight_col[:, None] * grads.astype(jnp.float32)).astype(jnp.bfloat16)
    hidden_grad = lax.dot_general(out_grad, down_weight, (((1,), (1,)), ((), ())), preferred_element_type=jnp.float32)
    gate_grad = (hidden_grad * up_value * sigmoid_gate * (1.0 + gate_value * (1.0 - sigmoid_gate))).astype(jnp.bfloat16)
    up_grad = (hidden_grad * silu_gate).astype(jnp.bfloat16)
    row_grads = lax.dot_general(gate_grad, gate_weight, (((1,), (1,)), ((), ())), preferred_element_type=jnp.float32)
    row_grads = row_grads + lax.dot_general(up_grad, up_weight, (((1,), (1,)), ((), ())), preferred_element_type=jnp.float32)
    partial_grad = lax.dot_general(hidden, out_grad, (((0,), (0,)), ((), ())), preferred_element_type=jnp.float32)
    return row_grads.astype(jnp.bfloat16), weight_slot, partial_grad.astype(jnp.bfloat16)


def reference(tokens, cotangent, expert_ids, route_weights, w_gate, w_up, w_down):
    per_replica = TOKENS // REPLICAS
    row_limit = GROUP_EXPERTS * SLOTS

    def expert_replica(carry, replica, expert_index):
        node_acc, weight_acc, grad_acc = carry
        base = (replica * per_replica).astype(jnp.int32)
        rep_tokens = lax.dynamic_slice_in_dim(tokens, base, per_replica, 0)
        rep_grads = lax.dynamic_slice_in_dim(cotangent, base, per_replica, 0)
        rep_ids = lax.dynamic_slice_in_dim(expert_ids, base, per_replica, 0)
        rep_weights = lax.dynamic_slice_in_dim(route_weights, base, per_replica, 0)
        hits = rep_ids == expert_index
        routed = jnp.any(hits, axis=1)
        positions = jnp.nonzero(routed, size=row_limit, fill_value=0)[0].astype(jnp.int32)
        filled = jnp.arange(row_limit, dtype=jnp.int32) < jnp.sum(routed.astype(jnp.int32))
        rows = jnp.where(filled[:, None], rep_tokens[positions], jnp.zeros((), rep_tokens.dtype))
        grads = jnp.where(filled[:, None], rep_grads[positions], jnp.zeros((), rep_grads.dtype))
        slot_weight = jnp.sum(jnp.where(hits, rep_weights.astype(jnp.float32), 0.0), axis=1)
        weight_col = jnp.where(filled, slot_weight[positions], 0.0)
        row_grads, weight_slot, partial_grad = expert_pass(rows, grads, weight_col, w_gate[expert_index], w_up[expert_index], w_down[expert_index])
        global_rows = base + positions
        node_acc = node_acc.at[global_rows].add(jnp.where(filled[:, None], row_grads.astype(jnp.float32), 0.0))
        slot_hits = hits[positions] & filled[:, None]
        weight_acc = weight_acc.at[global_rows].add(jnp.where(slot_hits, weight_slot.astype(jnp.float32)[:, None], 0.0))
        grad_acc = grad_acc + lax.optimization_barrier(partial_grad).astype(jnp.float32)
        return (node_acc, weight_acc, grad_acc), None

    def node_pass(carry, node):
        token_acc, weight_acc = carry

        def local_pass(inner, local):
            node_acc, weight_now = inner
            expert_index = (node * GROUP_EXPERTS + local).astype(jnp.int32)
            start_grad = jnp.zeros((FF, D), jnp.float32)

            def replica_step(state, replica):
                return expert_replica(state, replica, expert_index)

            (node_acc, weight_now, grad_acc), unused = lax.scan(replica_step, (node_acc, weight_now, start_grad), jnp.arange(REPLICAS, dtype=jnp.int32))
            return (node_acc, weight_now), grad_acc

        node_start = jnp.zeros((TOKENS, D), jnp.float32)
        (node_acc, weight_acc), grads = lax.scan(local_pass, (node_start, weight_acc), jnp.arange(GROUP_EXPERTS, dtype=jnp.int32))
        token_acc = token_acc + lax.optimization_barrier(node_acc.astype(jnp.bfloat16)).astype(jnp.float32)
        return (token_acc, weight_acc), grads

    start = (jnp.zeros((TOKENS, D), jnp.float32), jnp.zeros((TOKENS, TOP), jnp.float32))
    (token_acc, weight_acc), grads = lax.scan(node_pass, start, jnp.arange(NODE_GROUPS, dtype=jnp.int32))
    return token_acc.astype(jnp.bfloat16), weight_acc.astype(jnp.bfloat16), grads.reshape(EXPERTS, FF, D)
```

```python
import functools

import jax
import jax.numpy as jnp
from jax import lax
from jax.experimental import pallas as pl
from jax.experimental.pallas import tpu as pltpu
from jax.sharding import PartitionSpec as P

BF = jnp.bfloat16
F32 = jnp.float32
MESH = pl.DeviceIdType.MESH
LANES = 128
SLOT = 16
NT = (((1,), (1,)), ((), ()))


def near_first(count):
    return sorted(range(1, count), key=lambda j: (min(j, count - j), j))


def dot(a, b):
    return jnp.dot(a, b, preferred_element_type=F32)


def dot_nt(a, b):
    return lax.dot_general(a, b, NT, preferred_element_type=F32)


def kernel(
    sizes,
    tok_ref, cot_ref, ids_ref, rw_ref, wg_hbm, wu_hbm, wd_hbm,
    tg_ref, wgrad_ref, dg_ref,
    wg, wu, wd,
    col_t, col_c, sel_ref, selt_ref,
    send_t, recv_t, send_c, recv_c,
    fac_a, fac_b, hid, hid_t, out_g, gate_g, up_g, eo,
    send_b, recv_b, group, other, summed, home,
    rs_send, rs_recv,
    w_sem, xs_sem, xr_sem, fs_sem, ys_sem, yr_sem, zs_sem, zr_sem, cx_sem, hs_sem, hr_sem,
):
    nz, nn, nl = sizes
    nx = nn // 2
    toks, width = tok_ref.shape
    top = ids_ref.shape[1]
    half = width // 2
    quarter = width // 4
    hidden_units = wd.shape[0]
    chunk = hidden_units // nz
    slots = nl * SLOT
    rows = nn * SLOT
    tile = min(256, hidden_units)
    wide = min(256, half)

    z = lax.axis_index("edata")
    n = lax.axis_index("node")
    l = lax.axis_index("local")
    core = lax.rem(n, 2)
    x = lax.div(n, 2)
    mate = n + 1 - 2 * core
    expert = n * nl + l

    def node_at(j):
        return lax.rem(n + 2 * j, nn)

    def local_at(j):
        return lax.rem(l + j, nl)

    weights = [
        pltpu.make_async_copy(hbm.at[0], vmem, w_sem.at[i])
        for i, (hbm, vmem) in enumerate(((wg_hbm, wg), (wu_hbm, wu), (wd_hbm, wd)))
    ]
    for copy in weights:
        copy.start()

    barrier = pltpu.get_barrier_semaphore()
    for j in range(1, nx):
        pl.semaphore_signal(barrier, inc=1, device_id={"node": node_at(j)}, device_id_type=MESH)
    pl.semaphore_signal(barrier, inc=1, device_id={"node": mate}, device_id_type=MESH)
    for j in range(1, nl):
        pl.semaphore_signal(barrier, inc=1, device_id={"local": local_at(j)}, device_id_type=MESH)
    z_next = lax.rem(z + 1, nz)
    z_prev = lax.rem(z + nz - 1, nz)
    for peer in (z_next, z_prev):
        pl.semaphore_signal(barrier, inc=1, device_id={"edata": peer}, device_id_type=MESH)

    ids = ids_ref[...]
    lane = lax.broadcasted_iota(jnp.int32, (toks, LANES), 1)
    dense = jnp.zeros((toks, LANES), F32)
    for k in range(top):
        dense = dense + jnp.where(
            ids[:, k : k + 1] == lane, rw_ref[:, k : k + 1].astype(F32), 0.0
        )
    tok = tok_ref[...].astype(F32)
    cot = cot_ref[...].astype(F32)
    col_t[n, :, :half] = jnp.concatenate([tok[:, :half], tok[:, half:]], axis=0).astype(BF)
    col_t[n, :, half:] = jnp.concatenate([dense, jnp.zeros_like(dense)], axis=0).astype(BF)
    col_c[n, :, :] = jnp.concatenate([cot[:, :half], cot[:, half:]], axis=0).astype(BF)

    pl.semaphore_wait(barrier, nx - 1 + 1 + nl - 1 + 2)

    started = []

    def x_copy(which, src, target, send_sem):
        buf = (col_t, col_c)[which]
        return pltpu.make_async_remote_copy(
            src_ref=buf.at[src], dst_ref=buf.at[src],
            send_sem=send_sem, recv_sem=xr_sem.at[which, src],
            device_id={"node": target}, device_id_type=MESH,
        )

    order_x = near_first(nx)
    for which in range(2):
        for j in order_x:
            copy = x_copy(which, n, node_at(j), xs_sem.at[which, j])
            copy.start()
            started.append(copy)
        copy = x_copy(which, n, mate, xs_sem.at[which, 0])
        copy.start()
        started.append(copy)

    def spread(which):
        for j in order_x:
            src = node_at(nx - j)
            x_copy(which, src, mate, fs_sem.at[which, j]).wait_recv()
            copy = x_copy(which, src, mate, fs_sem.at[which, j])
            copy.start()
            started.append(copy)
        for j in [0] + order_x:
            src = lax.rem(mate + 2 * (nx - j), nn)
            x_copy(which, src, mate, fs_sem.at[which, j]).wait_recv()

    def y_copy(kind, src_buf, dst_buf, row, j, cols):
        return pltpu.make_async_remote_copy(
            src_ref=src_buf.at[pl.ds(pl.multiple_of(row * SLOT, SLOT), SLOT), cols],
            dst_ref=dst_buf.at[pl.ds(pl.multiple_of(l * SLOT, SLOT), SLOT), cols],
            send_sem=ys_sem.at[kind, j], recv_sem=yr_sem.at[kind, l],
            device_id={"local": row}, device_id_type=MESH,
        )

    order_y = near_first(nl)

    def y_send(kind, src_buf, dst_buf, cols):
        for j in order_y:
            copy = y_copy(kind, src_buf, dst_buf, local_at(j), j, cols)
            copy.start()
            started.append(copy)
        mine = pl.ds(pl.multiple_of(l * SLOT, SLOT), SLOT)
        dst_buf[mine, cols] = src_buf[mine, cols]

    def y_wait(kind, dst_buf, cols):
        for j in order_y:
            src = local_at(nl - j)
            part = dst_buf.at[pl.ds(pl.multiple_of(src * SLOT, SLOT), SLOT), cols]
            pltpu.make_async_remote_copy(
                src_ref=part, dst_ref=part, send_sem=ys_sem.at[kind, j],
                recv_sem=yr_sem.at[kind, src], device_id={"local": src}, device_id_type=MESH,
            ).wait_recv()

    left, right = slice(0, half), slice(half, width)
    right_ext = slice(half, width + LANES)
    all_ext = slice(0, width + LANES)

    spread(0)
    col_w = col_t[:, :, half:].reshape(rows, LANES)
    slot_id = lax.broadcasted_iota(jnp.int32, (slots, LANES), 0)
    lane_id = lax.broadcasted_iota(jnp.int32, (slots, LANES), 1)
    names = (lane_id == n * nl + lax.div(slot_id, SLOT)).astype(F32).astype(BF)
    named = dot_nt(names, col_w) != 0.0
    below = (
        lax.broadcasted_iota(jnp.int32, (rows, rows), 1)
        <= lax.broadcasted_iota(jnp.int32, (rows, rows), 0)
    ).astype(F32).astype(BF)
    count = dot_nt(named.astype(F32).astype(BF), below)
    place = lax.rem(lax.broadcasted_iota(jnp.int32, (slots, rows), 0), SLOT).astype(F32)
    sel0 = jnp.where(named & (count == place + 1.0), 1.0, 0.0)
    sel = jnp.concatenate([sel0, pltpu.roll(sel0, toks, 1)], axis=0)
    sel_ref[...] = sel.astype(BF)

    def pick(src_col, dst):
        for at in range(0, half, wide):
            got = dot(sel_ref[...], src_col[:, :, at : at + wide].reshape(rows, wide)).astype(BF)
            dst[:, at : at + wide] = got[:slots]
            dst[:, half + at : half + at + wide] = got[slots:]

    pick(col_t, send_t)
    send_t[:, width:] = dot(sel_ref[:slots, :], col_w).astype(BF)
    y_send(0, send_t, recv_t, all_ext)
    selt_ref[...] = sel.T.astype(BF)

    spread(1)
    pick(col_c, send_c)
    y_send(1, send_c, recv_c, left)
    y_send(2, send_c, recv_c, right)

    weights[0].wait()
    weights[1].wait()
    y_wait(0, recv_t, all_ext)
    for at in range(0, hidden_units, tile):
        cols = slice(at, at + tile)
        gate = dot(recv_t[:, :width], wg[:, cols])
        up = dot(recv_t[:, :width], wu[:, cols])
        sig = jax.nn.sigmoid(gate)
        silu = gate * sig
        fac_a[:, cols] = up * sig * (1.0 + gate * (1.0 - sig))
        fac_b[:, cols] = silu
        hidden = silu * up
        hid[:, cols] = hidden.astype(BF)
        hid_t[cols, :] = hidden.T.astype(BF)
    row_lane = lax.broadcasted_iota(jnp.int32, (slots, LANES), 1)
    scale = jnp.sum(
        jnp.where(row_lane == expert, recv_t[:, width:].astype(F32), 0.0), axis=1, keepdims=True
    )

    def scale_grads(cols):
        out_g[:, cols] = (scale * recv_c[:, cols].astype(F32)).astype(BF)

    def z_step(stream, step):
        ahead = stream % 2 == 0
        cols = slice(stream * quarter, (stream + 1) * quarter)
        part = lax.rem(z + 2 * nz - 1 - step, nz) if ahead else lax.rem(z + 1 + step, nz)

        def z_copy(at):
            return pltpu.make_async_remote_copy(
                src_ref=rs_send.at[stream, at], dst_ref=rs_recv.at[stream, at],
                send_sem=zs_sem.at[stream, at], recv_sem=zr_sem.at[stream, at],
                device_id={"edata": z_next if ahead else z_prev}, device_id_type=MESH,
            )

        own = dot(hid_t[pl.ds(pl.multiple_of(part * chunk, SLOT), chunk), :], out_g[:, cols])
        if step > 0:
            z_copy(step - 1).wait_recv()
            own = own + rs_recv[stream, step - 1].astype(F32)
        if step < nz - 1:
            rs_send[stream, step] = own.astype(BF)
            copy = z_copy(step)
            copy.start()
            started.append(copy)
        else:
            dg_ref[0, :, cols] = own

    y_wait(1, recv_c, left)
    scale_grads(left)
    z_step(0, 0)
    z_step(1, 0)
    y_wait(2, recv_c, right)
    scale_grads(right)
    z_step(2, 0)
    z_step(3, 0)

    weights[2].wait()
    for at in range(0, hidden_units, tile):
        cols = slice(at, at + tile)
        grad = dot_nt(out_g[...], wd[cols, :])
        gate_g[:, cols] = (grad * fac_a[:, cols]).astype(BF)
        up_g[:, cols] = (grad * fac_b[:, cols]).astype(BF)

    def row_grads(cols):
        for at in range(cols.start, cols.stop, wide):
            feats = slice(at, at + wide)
            send_b[:, feats] = (
                dot_nt(gate_g[...], wg[feats, :]) + dot_nt(up_g[...], wu[feats, :])
            ).astype(BF)

    pending = [(step, stream) for step in range(1, nz + 0) for stream in range(4)]

    def z_advance(count):
        for _ in range(count):
            if pending:
                step, stream = pending.pop(0)
                z_step(stream, step)

    row_grads(left)
    y_send(3, send_b, recv_b, left)
    z_advance(2)
    row_grads(right)
    weight_sum = jnp.zeros((slots, 1), F32)
    for at in range(0, width, wide):
        feats = slice(at, at + wide)
        out = dot(hid[...], wd[:, feats])
        weight_sum = weight_sum + jnp.sum(
            recv_c[:, feats].astype(F32) * out, axis=1, keepdims=True
        )
    send_b[:, width:] = jnp.where(row_lane == expert, weight_sum, 0.0).astype(BF)
    y_send(4, send_b, recv_b, right_ext)
    z_advance(10)

    y_wait(3, recv_b, left)
    y_wait(4, recv_b, right_ext)
    for at in range(0, half, wide):
        got = dot(selt_ref[:, :slots], recv_b[:, at : at + wide]) + dot(
            selt_ref[:, slots:], recv_b[:, half + at : half + at + wide]
        )
        group[:, :, :, at : at + wide] = got.astype(BF).reshape(nx, 2, SLOT, wide)
    group[:, :, :, half:] = (
        dot(selt_ref[:, :slots], recv_b[:, width:]).astype(BF).reshape(nx, 2, SLOT, LANES)
    )
    swap = pltpu.make_async_remote_copy(
        src_ref=group.at[:, 1 - core], dst_ref=other, send_sem=cx_sem.at[0], recv_sem=cx_sem.at[1],
        device_id={"node": mate}, device_id_type=MESH,
    )
    swap.start()
    z_advance(4)
    swap.wait()
    summed[...] = (group[:, core].astype(F32) + other[...].astype(F32)).astype(BF)

    def h_copy(target, j):
        return pltpu.make_async_remote_copy(
            src_ref=summed.at[target], dst_ref=home.at[x], send_sem=hs_sem.at[j],
            recv_sem=hr_sem.at[x], device_id={"node": 2 * target + core}, device_id_type=MESH,
        )

    for j in order_x:
        copy = h_copy(lax.rem(x + j, nx), j)
        copy.start()
        started.append(copy)
    home[x] = summed[x]
    z_advance(4)
    for j in order_x:
        src = lax.rem(x + nx - j, nx)
        pltpu.make_async_remote_copy(
            src_ref=home.at[src], dst_ref=home.at[src], send_sem=hs_sem.at[j],
            recv_sem=hr_sem.at[src], device_id={"node": 2 * src + core}, device_id_type=MESH,
        ).wait_recv()
    total = jnp.sum(home[...].astype(F32), axis=0)
    tg_ref[:, :half] = total[:toks, :half].astype(BF)
    tg_ref[:, half:] = total[toks:, :half].astype(BF)
    weight_dense = total[:toks, half:]
    slot_lane = lax.broadcasted_iota(jnp.int32, (toks, top), 1)
    weight_out = jnp.zeros((toks, top), F32)
    for k in range(top):
        value = jnp.sum(
            jnp.where(ids[:, k : k + 1] == lane, weight_dense, 0.0), axis=1, keepdims=True
        )
        weight_out = jnp.where(slot_lane == k, value, weight_out)
    wgrad_ref[...] = weight_out.astype(BF)
    z_advance(len(pending))
    for copy in started:
        copy.wait_send()


def body(tokens, cotangent, expert_ids, route_weights, w_gate, w_up, w_down):
    nz, nn, nl = (lax.axis_size(name) for name in ("edata", "node", "local"))
    nx = nn // 2
    toks, width = tokens.shape
    top = expert_ids.shape[1]
    hidden_units = w_gate.shape[2]
    half, quarter, chunk = width // 2, width // 4, hidden_units // nz
    slots, rows = nl * SLOT, nn * SLOT
    vmem = pl.BlockSpec(memory_space=pltpu.VMEM)
    hbm = pl.BlockSpec(memory_space=pl.ANY)
    dma = pltpu.SemaphoreType.DMA
    return pl.pallas_call(
        functools.partial(kernel, (nz, nn, nl)),
        out_shape=(
            jax.ShapeDtypeStruct((toks, width), BF),
            jax.ShapeDtypeStruct((toks, top), BF),
            jax.ShapeDtypeStruct((1, chunk, width), F32),
        ),
        in_specs=[vmem, vmem, vmem, vmem, hbm, hbm, hbm],
        out_specs=(vmem, vmem, vmem),
        scratch_shapes=[
            pltpu.VMEM((width, hidden_units), BF),
            pltpu.VMEM((width, hidden_units), BF),
            pltpu.VMEM((hidden_units, width), BF),
            pltpu.VMEM((nn, SLOT, half + LANES), BF),
            pltpu.VMEM((nn, SLOT, half), BF),
            pltpu.VMEM((2 * slots, rows), BF),
            pltpu.VMEM((rows, 2 * slots), BF),
            pltpu.VMEM((slots, width + LANES), BF),
            pltpu.VMEM((slots, width + LANES), BF),
            pltpu.VMEM((slots, width), BF),
            pltpu.VMEM((slots, width), BF),
            pltpu.VMEM((slots, hidden_units), F32),
            pltpu.VMEM((slots, hidden_units), F32),
            pltpu.VMEM((slots, hidden_units), BF),
            pltpu.VMEM((hidden_units, slots), BF),
            pltpu.VMEM((slots, width), BF),
            pltpu.VMEM((slots, hidden_units), BF),
            pltpu.VMEM((slots, hidden_units), BF),
            pltpu.VMEM((8, LANES), F32),
            pltpu.VMEM((slots, width + LANES), BF),
            pltpu.VMEM((slots, width + LANES), BF),
            pltpu.VMEM((nx, 2, SLOT, half + LANES), BF),
            pltpu.VMEM((nx, SLOT, half + LANES), BF),
            pltpu.VMEM((nx, SLOT, half + LANES), BF),
            pltpu.VMEM((nx, SLOT, half + LANES), BF),
            pltpu.VMEM((4, nz - 1, chunk, quarter), BF),
            pltpu.VMEM((4, nz - 1, chunk, quarter), BF),
            dma((3,)),
            dma((2, nx)),
            dma((2, nn)),
            dma((2, nx)),
            dma((5, nl)),
            dma((5, nl)),
            dma((4, nz - 1)),
            dma((4, nz - 1)),
            dma((2,)),
            dma((nx,)),
            dma((nx,)),
        ],
        compiler_params=pltpu.CompilerParams(
            collective_id=0, has_side_effects=True, vmem_limit_bytes=48 * 1024 * 1024
        ),
        name="expert_layer",
    )(tokens, cotangent, expert_ids, route_weights, w_gate, w_up, w_down)


def solution(mesh):
    in_specs = (
        P(("edata", "node", "local"), None),
        P(("edata", "node", "local"), None),
        P(("edata", "node", "local"), None),
        P(("edata", "node", "local"), None),
        P(("node", "local"), None, None),
        P(("node", "local"), None, None),
        P(("node", "local"), None, None),
    )
    out_specs = (
        P(("edata", "node", "local"), None),
        P(("edata", "node", "local"), None),
        P(("node", "local"), "edata", None),
    )
    return jax.shard_map(body, mesh=mesh, in_specs=in_specs, out_specs=out_specs, check_vma=False)
```

```python
import functools

import jax
import jax.numpy as jnp
from jax import lax
from jax.experimental import pallas as pl
from jax.experimental.pallas import tpu as pltpu
from jax.sharding import PartitionSpec as P

BF = jnp.bfloat16
F32 = jnp.float32
MESH = pl.DeviceIdType.MESH
LANES = 128
SLOT = 16
NT = (((1,), (1,)), ((), ()))


def near_first(count):
    return sorted(range(1, count), key=lambda j: (min(j, count - j), j))


def dot(a, b):
    return jnp.dot(a, b, preferred_element_type=F32)


def dot_nt(a, b):
    return lax.dot_general(a, b, NT, preferred_element_type=F32)


def kernel(
    sizes,
    tok_hbm, cot_hbm, ids_hbm, rw_hbm, wg_hbm, wu_hbm, wd_hbm,
    tg_ref, wgrad_ref, dg_ref,
    tok_ref, cot_ref, ids_ref, rw_ref, wg, wu, wd,
    col_t, col_c, sel_ref, selt_ref,
    send_t, recv_t, send_c, recv_c,
    fac_a, fac_b, hid, hid_t, out_g, gate_g, up_g, hid_g,
    send_b, recv_b, group, other, summed, home,
    partial, rs_send, rs_recv,
    w_sem, xs_sem, xr_sem, fs_sem, ys_sem, yr_sem, zs_sem, zr_sem, cx_sem, hs_sem, hr_sem,
):
    nz, nn, nl = sizes
    nx = nn // 2
    toks, width = tok_ref.shape
    top = ids_ref.shape[1]
    half = width // 2
    quarter = width // 4
    lead = half // 4
    hidden_units = wd.shape[0]
    chunk = hidden_units // nz
    slots = nl * SLOT
    rows = nn * SLOT
    tile = min(256, hidden_units)
    wide = min(256, half)

    z = lax.axis_index("edata")
    n = lax.axis_index("node")
    l = lax.axis_index("local")
    core = lax.rem(n, 2)
    x = lax.div(n, 2)
    mate = n + 1 - 2 * core
    expert = n * nl + l

    def node_at(j):
        return lax.rem(n + 2 * j, nn)

    def local_at(j):
        return lax.rem(l + j, nl)

    inputs = [
        pltpu.make_async_copy(hbm, vmem, w_sem.at[i])
        for i, (hbm, vmem) in enumerate((
            (ids_hbm, ids_ref), (rw_hbm, rw_ref), (tok_hbm, tok_ref), (cot_hbm, cot_ref),
            (wg_hbm.at[0], wg), (wu_hbm.at[0], wu), (wd_hbm.at[0], wd),
        ))
    ]
    for copy in inputs:
        copy.start()
    weights = inputs[4:]

    barrier = pltpu.get_barrier_semaphore()
    for j in range(1, nx):
        pl.semaphore_signal(barrier, inc=1, device_id={"node": node_at(j)}, device_id_type=MESH)
    pl.semaphore_signal(barrier, inc=1, device_id={"node": mate}, device_id_type=MESH)
    for j in range(1, nl):
        pl.semaphore_signal(barrier, inc=1, device_id={"local": local_at(j)}, device_id_type=MESH)
    z_next = lax.rem(z + 1, nz)
    z_prev = lax.rem(z + nz - 1, nz)
    for peer in (z_next, z_prev):
        pl.semaphore_signal(barrier, inc=1, device_id={"edata": peer}, device_id_type=MESH)

    for copy in inputs[:4]:
        copy.wait()
    ids = ids_ref[...]
    lane = lax.broadcasted_iota(jnp.int32, (toks, LANES), 1)
    dense = jnp.zeros((toks, LANES), F32)
    for k in range(top):
        dense = dense + jnp.where(
            ids[:, k : k + 1] == lane, rw_ref[:, k : k + 1].astype(F32), 0.0
        )
    tok = tok_ref[...].astype(F32)
    cot = cot_ref[...].astype(F32)
    col_t[n, :, LANES:] = jnp.concatenate([tok[:, :half], tok[:, half:]], axis=0).astype(BF)
    col_t[n, :, :LANES] = jnp.concatenate([dense, jnp.zeros_like(dense)], axis=0).astype(BF)
    col_c[n, :, :] = jnp.concatenate([cot[:, :half], cot[:, half:]], axis=0).astype(BF)

    pl.semaphore_wait(barrier, nx - 1 + 1 + nl - 1 + 2)

    started = []

    x_parts = [
        col_t.at[:, :, : LANES + lead],
        col_t.at[:, :, LANES + lead :],
        col_c,
    ]

    def x_copy(which, src, target, send_sem):
        block = x_parts[which].at[src]
        return pltpu.make_async_remote_copy(
            src_ref=block, dst_ref=block,
            send_sem=send_sem, recv_sem=xr_sem.at[which, src],
            device_id={"node": target}, device_id_type=MESH,
        )

    order_x = near_first(nx)

    def x_send(which):
        for j in order_x:
            copy = x_copy(which, n, node_at(j), xs_sem.at[which, j])
            copy.start()
            started.append(copy)
        copy = x_copy(which, n, mate, xs_sem.at[which, 0])
        copy.start()
        started.append(copy)

    def spread(which):
        for j in order_x:
            src = node_at(nx - j)
            x_copy(which, src, mate, fs_sem.at[which, j]).wait_recv()
            copy = x_copy(which, src, mate, fs_sem.at[which, j])
            copy.start()
            started.append(copy)
        for j in [0] + order_x:
            src = lax.rem(mate + 2 * (nx - j), nn)
            x_copy(which, src, mate, fs_sem.at[which, j]).wait_recv()

    x_send(0)
    x_send(1)

    def y_copy(kind, src_buf, dst_buf, row, j, cols):
        return pltpu.make_async_remote_copy(
            src_ref=src_buf.at[pl.ds(pl.multiple_of(row * SLOT, SLOT), SLOT), cols],
            dst_ref=dst_buf.at[pl.ds(pl.multiple_of(l * SLOT, SLOT), SLOT), cols],
            send_sem=ys_sem.at[kind, j], recv_sem=yr_sem.at[kind, l],
            device_id={"local": row}, device_id_type=MESH,
        )

    order_y = near_first(nl)

    def y_send(kind, src_buf, dst_buf, cols):
        for j in order_y:
            copy = y_copy(kind, src_buf, dst_buf, local_at(j), j, cols)
            copy.start()
            started.append(copy)
        mine = pl.ds(pl.multiple_of(l * SLOT, SLOT), SLOT)
        dst_buf[mine, cols] = src_buf[mine, cols]

    def y_wait(kind, dst_buf, cols):
        for j in order_y:
            src = local_at(nl - j)
            part = dst_buf.at[pl.ds(pl.multiple_of(src * SLOT, SLOT), SLOT), cols]
            pltpu.make_async_remote_copy(
                src_ref=part, dst_ref=part, send_sem=ys_sem.at[kind, j],
                recv_sem=yr_sem.at[kind, src], device_id={"local": src}, device_id_type=MESH,
            ).wait_recv()

    parts = [slice(i * quarter, (i + 1) * quarter) for i in (0, 2, 1, 3)]
    back_parts = parts[:3] + [slice(parts[3].start, width + LANES)]
    lead_cols, rest_cols = slice(0, LANES + 2 * lead), slice(LANES + 2 * lead, LANES + width)

    spread(0)
    col_w = col_t[:, :, :LANES].reshape(rows, LANES)
    slot_id = lax.broadcasted_iota(jnp.int32, (slots, LANES), 0)
    lane_id = lax.broadcasted_iota(jnp.int32, (slots, LANES), 1)
    names = (lane_id == n * nl + lax.div(slot_id, SLOT)).astype(F32).astype(BF)
    named = dot_nt(names, col_w) != 0.0
    below = (
        lax.broadcasted_iota(jnp.int32, (rows, rows), 1)
        <= lax.broadcasted_iota(jnp.int32, (rows, rows), 0)
    ).astype(F32).astype(BF)
    count = dot_nt(named.astype(F32).astype(BF), below)
    place = lax.rem(lax.broadcasted_iota(jnp.int32, (slots, rows), 0), SLOT).astype(F32)
    sel0 = jnp.where(named & (count == place + 1.0), 1.0, 0.0)
    sel = jnp.concatenate([sel0, pltpu.roll(sel0, toks, 1)], axis=0)
    sel_ref[...] = sel.astype(BF)

    def pick(src_col, at, size, dst, first, second):
        for i in range(0, size, lead):
            got = src_col[:, :, at + i : at + i + lead].reshape(rows, lead)
            got = dot(sel_ref[...], got).astype(BF)
            dst[:, first + i : first + i + lead] = got[:slots]
            dst[:, second + i : second + i + lead] = got[slots:]

    send_t[:, :LANES] = dot(sel_ref[:slots, :], col_w).astype(BF)
    pick(col_t, LANES, lead, send_t, LANES, LANES + lead)
    y_send(0, send_t, recv_t, lead_cols)
    spread(1)
    x_send(2)
    rest = half - lead
    pick(col_t, LANES + lead, rest, send_t, LANES + 2 * lead, LANES + 2 * lead + rest)
    y_send(9, send_t, recv_t, rest_cols)
    selt_ref[...] = sel.T.astype(BF)

    spread(2)
    pick(col_c, 0, quarter, send_c, 0, half)
    y_send(1, send_c, recv_c, parts[0])
    y_send(2, send_c, recv_c, parts[1])
    pick(col_c, quarter, quarter, send_c, quarter, half + quarter)
    y_send(3, send_c, recv_c, parts[2])
    y_send(4, send_c, recv_c, parts[3])

    weights[0].wait()
    weights[1].wait()
    y_wait(0, recv_t, lead_cols)
    y_wait(9, recv_t, rest_cols)
    row_parts = [
        (LANES, 0, lead),
        (LANES + lead, half, lead),
        (LANES + 2 * lead, lead, rest),
        (LANES + 2 * lead + rest, half + lead, rest),
    ]
    for at in range(0, hidden_units, tile):
        cols = slice(at, at + tile)
        gate = jnp.zeros((slots, tile), F32)
        up = jnp.zeros((slots, tile), F32)
        for first, feat, size in row_parts:
            got = recv_t[:, first : first + size]
            gate = gate + dot(got, wg[feat : feat + size, cols])
            up = up + dot(got, wu[feat : feat + size, cols])
        sig = jax.nn.sigmoid(gate)
        silu = gate * sig
        fac_a[:, cols] = up * sig * (1.0 + gate * (1.0 - sig))
        fac_b[:, cols] = silu
        hidden = silu * up
        hid[:, cols] = hidden.astype(BF)
        hid_t[cols, :] = hidden.T.astype(BF)
    row_lane = lax.broadcasted_iota(jnp.int32, (slots, LANES), 1)
    scale = jnp.sum(
        jnp.where(row_lane == expert, recv_t[:, :LANES].astype(F32), 0.0), axis=1, keepdims=True
    )
    weights[2].wait()

    def z_step(stream, step):
        ahead = stream % 2 == 0
        cols = parts[stream]
        part = lax.rem(z + 2 * nz - 1 - step, nz) if ahead else lax.rem(z + 1 + step, nz)
        own = partial.at[pl.ds(pl.multiple_of(part * chunk, SLOT), chunk), cols]

        def z_copy(at):
            return pltpu.make_async_remote_copy(
                src_ref=own if at == 0 else rs_send.at[stream, at - 1], dst_ref=rs_recv.at[stream, at],
                send_sem=zs_sem.at[stream, at], recv_sem=zr_sem.at[stream, at],
                device_id={"edata": z_next if ahead else z_prev}, device_id_type=MESH,
            )

        if step > 0:
            z_copy(step - 1).wait_recv()
        if step == nz - 1:
            dg_ref[0, :, cols] = rs_recv[stream, step - 1].astype(F32) + own[...].astype(F32)
            return
        if step > 0:
            rs_send[stream, step - 1] = rs_recv[stream, step - 1] + own[...]
        copy = z_copy(step)
        copy.start()
        started.append(copy)

    done = [0] * 4

    def z_advance(upto, streams=(0, 1, 2, 3)):
        for step in range(min(upto, nz)):
            for stream in streams:
                if done[stream] == step:
                    z_step(stream, step)
                    done[stream] += 1

    weight_sum = jnp.zeros((slots, 1), F32)
    for i, cols in enumerate(parts):
        y_wait(1 + i, recv_c, cols)
        out_g[:, cols] = (scale * recv_c[:, cols].astype(F32)).astype(BF)
        for at in range(0, hidden_units, tile):
            units = slice(at, at + tile)
            partial[units, cols] = dot(hid_t[units, :], out_g[:, cols]).astype(BF)
        z_advance(1, (i,))
        if i == 2:
            z_advance(2, (0,))
        if i == 3:
            z_advance(2, (1,))
        for at in range(0, hidden_units, tile):
            units = slice(at, at + tile)
            grad = dot_nt(out_g[:, cols], wd[units, cols])
            if i > 0:
                grad = grad + hid_g[:, units]
            if i < 3:
                hid_g[:, units] = grad
            else:
                gate_g[:, units] = (grad * fac_a[:, units]).astype(BF)
                up_g[:, units] = (grad * fac_b[:, units]).astype(BF)
        out = dot(hid[...], wd[:, cols])
        weight_sum = weight_sum + jnp.sum(
            recv_c[:, cols].astype(F32) * out, axis=1, keepdims=True
        )

    for i, cols in enumerate(parts):
        for at in range(cols.start, cols.stop, min(wide, quarter)):
            feats = slice(at, at + min(wide, quarter))
            send_b[:, feats] = (
                dot_nt(gate_g[...], wg[feats, :]) + dot_nt(up_g[...], wu[feats, :])
            ).astype(BF)
        if i == 3:
            send_b[:, width:] = jnp.where(row_lane == expert, weight_sum, 0.0).astype(BF)
        y_send(5 + i, send_b, recv_b, back_parts[i])
        if i == 0:
            z_advance(2)
        if i == 2:
            z_advance(3)
    z_advance(4)

    home_cols = [slice(0, quarter), slice(quarter, half + LANES)]

    def gather_group(i):
        y_wait(5 + 2 * i, recv_b, back_parts[2 * i])
        y_wait(6 + 2 * i, recv_b, back_parts[2 * i + 1])
        at, end = i * quarter, (i + 1) * quarter
        got = dot(selt_ref[:, :slots], recv_b[:, at:end]) + dot(
            selt_ref[:, slots:], recv_b[:, half + at : half + end]
        )
        group[:, :, :, at:end] = got.astype(BF).reshape(nx, 2, SLOT, quarter)
        if i == 1:
            group[:, :, :, half:] = (
                dot(selt_ref[:, :slots], recv_b[:, width:]).astype(BF).reshape(nx, 2, SLOT, LANES)
            )
        cols = home_cols[i]
        swap = pltpu.make_async_remote_copy(
            src_ref=group.at[:, 1 - core, :, cols], dst_ref=other.at[:, :, cols],
            send_sem=cx_sem.at[i, 0], recv_sem=cx_sem.at[i, 1],
            device_id={"node": mate}, device_id_type=MESH,
        )
        swap.start()
        return swap

    def send_home(i, swap):
        cols = home_cols[i]
        swap.wait()
        summed[:, :, cols] = (
            group[:, core, :, cols].astype(F32) + other[:, :, cols].astype(F32)
        ).astype(BF)
        for j in order_x:
            target = lax.rem(x + j, nx)
            copy = pltpu.make_async_remote_copy(
                src_ref=summed.at[target, :, cols], dst_ref=home.at[x, :, cols],
                send_sem=hs_sem.at[i, j], recv_sem=hr_sem.at[i, x],
                device_id={"node": 2 * target + core}, device_id_type=MESH,
            )
            copy.start()
            started.append(copy)
        home[x, :, cols] = summed[x, :, cols]

    def home_sum(i):
        cols = home_cols[i]
        for j in order_x:
            src = lax.rem(x + nx - j, nx)
            part = home.at[src, :, cols]
            pltpu.make_async_remote_copy(
                src_ref=part, dst_ref=part, send_sem=hs_sem.at[i, j],
                recv_sem=hr_sem.at[i, src], device_id={"node": 2 * src + core},
                device_id_type=MESH,
            ).wait_recv()
        total = jnp.sum(home[:, :, cols].astype(F32), axis=0)
        at = i * quarter
        tg_ref[:, at : at + quarter] = total[:toks, :quarter].astype(BF)
        tg_ref[:, half + at : half + at + quarter] = total[toks:, :quarter].astype(BF)
        return total[:toks, quarter:]

    swap = gather_group(0)
    z_advance(5)
    send_home(0, swap)
    z_advance(6)
    swap = gather_group(1)
    z_advance(7)
    send_home(1, swap)
    home_sum(0)
    z_advance(8)
    weight_dense = home_sum(1)
    slot_lane = lax.broadcasted_iota(jnp.int32, (toks, top), 1)
    weight_out = jnp.zeros((toks, top), F32)
    for k in range(top):
        value = jnp.sum(
            jnp.where(ids[:, k : k + 1] == lane, weight_dense, 0.0), axis=1, keepdims=True
        )
        weight_out = jnp.where(slot_lane == k, value, weight_out)
    wgrad_ref[...] = weight_out.astype(BF)
    for copy in started:
        copy.wait_send()


def body(tokens, cotangent, expert_ids, route_weights, w_gate, w_up, w_down):
    nz, nn, nl = (lax.axis_size(name) for name in ("edata", "node", "local"))
    nx = nn // 2
    toks, width = tokens.shape
    top = expert_ids.shape[1]
    hidden_units = w_gate.shape[2]
    half, quarter, chunk = width // 2, width // 4, hidden_units // nz
    slots, rows = nl * SLOT, nn * SLOT
    vmem = pl.BlockSpec(memory_space=pltpu.VMEM)
    hbm = pl.BlockSpec(memory_space=pltpu.HBM)
    dma = pltpu.SemaphoreType.DMA
    return pl.pallas_call(
        functools.partial(kernel, (nz, nn, nl)),
        out_shape=(
            jax.ShapeDtypeStruct((toks, width), BF),
            jax.ShapeDtypeStruct((toks, top), BF),
            jax.ShapeDtypeStruct((1, chunk, width), F32),
        ),
        in_specs=[hbm] * 7,
        out_specs=(vmem, vmem, vmem),
        scratch_shapes=[
            pltpu.VMEM((toks, width), BF),
            pltpu.VMEM((toks, width), BF),
            pltpu.VMEM((toks, top), jnp.int32),
            pltpu.VMEM((toks, top), BF),
            pltpu.VMEM((width, hidden_units), BF),
            pltpu.VMEM((width, hidden_units), BF),
            pltpu.VMEM((hidden_units, width), BF),
            pltpu.VMEM((nn, SLOT, half + LANES), BF),
            pltpu.VMEM((nn, SLOT, half), BF),
            pltpu.VMEM((2 * slots, rows), BF),
            pltpu.VMEM((rows, 2 * slots), BF),
            pltpu.VMEM((slots, width + LANES), BF),
            pltpu.VMEM((slots, width + LANES), BF),
            pltpu.VMEM((slots, width), BF),
            pltpu.VMEM((slots, width), BF),
            pltpu.VMEM((slots, hidden_units), F32),
            pltpu.VMEM((slots, hidden_units), F32),
            pltpu.VMEM((slots, hidden_units), BF),
            pltpu.VMEM((hidden_units, slots), BF),
            pltpu.VMEM((slots, width), BF),
            pltpu.VMEM((slots, hidden_units), BF),
            pltpu.VMEM((slots, hidden_units), BF),
            pltpu.VMEM((slots, hidden_units), F32),
            pltpu.VMEM((slots, width + LANES), BF),
            pltpu.VMEM((slots, width + LANES), BF),
            pltpu.VMEM((nx, 2, SLOT, half + LANES), BF),
            pltpu.VMEM((nx, SLOT, half + LANES), BF),
            pltpu.VMEM((nx, SLOT, half + LANES), BF),
            pltpu.VMEM((nx, SLOT, half + LANES), BF),
            pltpu.VMEM((hidden_units, width), BF),
            pltpu.VMEM((4, nz - 2, chunk, quarter), BF),
            pltpu.VMEM((4, nz - 1, chunk, quarter), BF),
            dma((7,)),
            dma((3, nx)),
            dma((3, nn)),
            dma((3, nx)),
            dma((10, nl)),
            dma((10, nl)),
            dma((4, nz - 1)),
            dma((4, nz - 1)),
            dma((2, 2)),
            dma((2, nx)),
            dma((2, nx)),
        ],
        compiler_params=pltpu.CompilerParams(
            collective_id=0, has_side_effects=True, vmem_limit_bytes=58 * 1024 * 1024
        ),
        name="expert_layer",
    )(tokens, cotangent, expert_ids, route_weights, w_gate, w_up, w_down)


def solution(mesh):
    in_specs = (
        P(("edata", "node", "local"), None),
        P(("edata", "node", "local"), None),
        P(("edata", "node", "local"), None),
        P(("edata", "node", "local"), None),
        P(("node", "local"), None, None),
        P(("node", "local"), None, None),
        P(("node", "local"), None, None),
    )
    out_specs = (
        P(("edata", "node", "local"), None),
        P(("edata", "node", "local"), None),
        P(("node", "local"), "edata", None),
    )
    return jax.shard_map(body, mesh=mesh, in_specs=in_specs, out_specs=out_specs, check_vma=False)
```
